32 devices in a mesh: group: 2 (over y), expert: 4 (over z), tensor: 4 (over x, core).
Axes of the slice: x: 2, y: 2, z: 4, core: 2. Of those that a mesh axis runs over, the one named last changes fastest.
Arguments:
- stream: bfloat16 [2, 8, 384, 4096], P(None, ('group', 'expert'), 'tensor'), parts along dimension 1, may hold values from -6 to 6
- queries: bfloat16 [2, 8, 384, 4096], P(None, ('group', 'expert'), None, 'tensor'), parts along dimension 1, may hold values from -160 to 160
- key_rows: bfloat16 [2, 8, 384, 256], P(None, ('group', 'expert'), 'tensor'), parts along dimension 1, may hold values from -4 to 4
- value_rows: bfloat16 [2, 8, 384, 256], P(None, ('group', 'expert'), 'tensor'), parts along dimension 1, may hold values from -6 to 6
- segments: int32 [2, 8, 384], P(None, ('group', 'expert')), parts along dimension 1, may hold values from 0 to 1, never falling along the last dimension, each value on 1 to 288 neighbouring positions
- out_proj: bfloat16 [4096, 4096], P('tensor', 'expert'), may hold values from -0.09375 to 0.09375
- norm_gain: float32 [4096], replicated, may hold values from 0.1 to 1.9
- router: bfloat16 [4096, 8], replicated, may hold values from -0.09375 to 0.09375
- routes: int32 [2, 8, 384, 2], P(None, ('group', 'expert'), 'tensor'), parts along dimension 1, may hold values from 0 to 7, all different within a row; in each aligned block of 96 rows (0 to 95, 96 to 191, ..., all dimensions but the last counted through in order) at most 36 rows name the same one
- gate_proj: bfloat16 [16, 4096, 384], P(('expert', 'tensor')), may hold values from -0.09375 to 0.09375
- up_proj: bfloat16 [16, 4096, 384], P(('expert', 'tensor')), may hold values from -0.09375 to 0.09375
- down_proj: bfloat16 [16, 384, 4096], P(('expert', 'tensor')), may hold values from -0.21875 to 0.21875
Outputs:
- layer_out: bfloat16 [2, 8, 384, 4096], P(None, ('group', 'expert'), 'tensor'), parts along dimension 1
The draws below stay inside these ranges and needn't reach their ends.
There are 2 independent parts, one for each index of `group`. The reference program is written for one: setup_inputs(seed, part) draws one part's arguments, and reference() takes and returns one part's arrays. A program takes and returns all parts, laid end to end along the dimension named above; an argument that names none is the same for every part. Nothing has to cross between parts.
Inputs may be any that keep to these rules, and one draw needn't show every extreme that they name: `routes`: each row names 2 different experts. Within the rows of one device in one micro-batch (aligned blocks of 96 rows) no expert is named more than 36 times, a bound that some block reaches. `segments`: within each micro-batch of a request group the document numbers never fall; each document holds 1 to 288 tokens.
All inputs are finite; a program needn't handle non-finite values.
Results may differ from the reference program's by a relative error of at most 0.0095.
Values may be sent and summed in bfloat16 or wider, within the bound.
A program may use at most 128 MiB of HBM per device.

```python
import math
from functools import partial
import jax
import jax.numpy as jnp
import numpy as np
from jax import lax

D = 4096
HEADS = 32
KV = 2
HD = 128
FF = 768
TOPK = 2
MICRO = 2
DOCS = 2
MB_TOK = 96
GROUPS = 4
MB = 384
EXPERTS = 8
HALF = 384
CAP = 36
N_TENSOR = 4


def shared_keys(key):
    base = jax.random.normal(key, (MICRO, GROUPS, MB, KV * HD), jnp.float32)
    return jnp.clip(base, -4.0, 4.0)


def draw_key_rows(key, part):
    base = shared_keys(key)
    return base.astype(jnp.bfloat16)


def draw_queries(key, part):
    key = jax.random.fold_in(key, 23)
    drawn = jax.random.normal(key, (MICRO, GROUPS, MB, HEADS * HD), jnp.float32)
    return jnp.clip(drawn, -160.0, 160.0).astype(jnp.bfloat16)


def block_levels(key, dims, split, least, top_value):
    gain = 1.0
    for position, shards_of in split:
        draws = jax.random.uniform(jax.random.fold_in(jax.random.fold_in(key, 6), position), (shards_of,), jnp.float32, least / len(split), top_value / len(split))
        gain = gain * jnp.repeat(jnp.exp(draws), dims[position] // shards_of).reshape((-1,) + (1,) * (len(dims) - 1 - position))
    return gain


def profile(count, total, bound, slope):
    loads = [(1 << 20) // math.isqrt(standing ** slope) + 1 for standing in range(2, count + 1)]
    rest, counts = total - bound - (count - 1), [1] * (count - 1)
    while rest > 0:
        free = [i for i in range(count - 1) if counts[i] < bound]
        whole, left = sum([loads[i] for i in free]), rest
        for i in free:
            extra = min(bound - counts[i], max(1, left * loads[i] // whole), rest)
            counts[i] = counts[i] + extra
            rest = rest - extra
    return np.array([bound] + counts)


def ragged(key, count, total, most, skew):
    if count == 2:
        one = jax.random.randint(key, (), max(1, total - most), min(most, total - 1) + 1)
        return jnp.stack([one, total - one])
    tallies = jnp.asarray(profile(count, total, most, skew), jnp.int32)
    couples = (count - 1) // 2
    giver, sink = tallies[1:1 + 2 * couples:2], tallies[2:2 + 2 * couples:2]
    room = jnp.minimum(giver - 1, most - sink)
    passed = jax.random.randint(jax.random.fold_in(key, 1), (couples,), 0, 1 << 20) % (room + 1)
    tallies = tallies.at[1:1 + 2 * couples:2].set(giver - passed).at[2:2 + 2 * couples:2].set(sink + passed)
    return tallies[jax.random.permutation(jax.random.fold_in(key, 2), count)]


def assign_block(rng, own, number, rows, number_of, top, bound, skew):
    sequence = jax.random.permutation(rng, number_of)
    heavy_load, usual = portions_of(number_of, rows * top, bound, skew, True), portions_of(number_of, rows * top, bound, skew, False)
    places = jnp.arange(number_of)

    def named(sizes, turn):
        used = int((sizes > 0).sum())
        fixed = max(1, used // 4)
        shifted = fixed + (places - fixed + turn * (used - fixed)) % max(1, number_of - fixed)
        return jnp.zeros((number_of,), jnp.int32).at[sequence[jnp.where(places < fixed, places, shifted)]].set(jnp.asarray(sizes, jnp.int32))

    sizes = jnp.where(number % 4 == 0, named(heavy_load, number // 4), named(usual, number - number // 4 - 1))
    mixed = jax.random.permutation(jax.random.fold_in(own, 3), number_of)
    donor, taker = mixed[0:number_of // 2 * 2:2], mixed[1:number_of // 2 * 2:2]
    slack = jnp.minimum(sizes[donor] - 1, bound - sizes[taker]) // 2
    slack = jnp.where((donor == sequence[0]) | (taker == sequence[0]) | (sizes[taker] == 0), 0, jnp.maximum(slack, 0))
    shifted = jax.random.randint(jax.random.fold_in(own, 4), (number_of // 2,), 0, 1 << 20) % (slack + 1)
    sizes = sizes.at[donor].add(-shifted).at[taker].add(shifted)
    labels = jnp.searchsorted(jnp.cumsum(sizes), jnp.arange(rows * top), side="right").astype(jnp.int32)
    listing = labels.reshape(top, rows).T
    listing = listing[jax.random.permutation(jax.random.fold_in(own, 1), rows)]
    turn = jax.random.randint(jax.random.fold_in(own, 2), (rows, 1), 0, top)
    return jnp.take_along_axis(listing, (jnp.arange(top)[None, :] + turn) % top, axis=1)


def portions_of(count, total, most, skew, full):
    loads = [(1 << 20) // math.isqrt(grade ** skew) + 1 for grade in range(1, count + 1)]
    largest = most if full else min(most, max(-(-total // count), total * loads[0] // sum(loads)))
    least = 1 if total - largest >= count - 1 else 0
    counts, spare = [largest] + [least] * (count - 1), total - largest - least * (count - 1)
    while spare > 0:
        free = [i for i in range(1, count) if counts[i] < largest] or [i for i in range(1, count) if counts[i] < most]
        pool, remaining = sum([loads[i] for i in free]), spare
        for i in free:
            addition = min(most - counts[i], max(1, remaining * loads[i] // pool), spare)
            counts[i] = counts[i] + addition
            spare = spare - addition
    return np.array(counts)


def scatter_about(key, dims, scale, most, shards=(), kind=jnp.bfloat16):
    factor_of = block_levels(key, dims, shards, -0.22, 0.18) if shards else 1.0
    values = jax.random.normal(key, dims, jnp.float32) * scale * factor_of
    return jnp.minimum(jnp.maximum(values, -most), most).astype(kind)


def setup_inputs(seed: int = 0, part: int = 0) -> dict:
    streams_of = jax.random.split(jax.random.key(seed), 13)
    own_keys = jax.random.split(jax.random.fold_in(streams_of[12], part), 13)
    stream = scatter_about(own_keys[0], (MICRO, GROUPS, MB, D), 1.0, 6.0, ((1, 4), (2, 4)))
    queries = draw_queries(jax.random.fold_in(jax.random.fold_in(streams_of[12], part), 71), part)
    key_rows = draw_key_rows(jax.random.fold_in(jax.random.fold_in(streams_of[12], part), 71), part)
    value_rows = scatter_about(own_keys[3], (MICRO, GROUPS, MB, KV * HD), 1.0, 6.0, ((1, 4), (2, 4)))
    segments = jax.vmap(lambda own: jnp.searchsorted(jnp.cumsum(ragged(own, DOCS, MB, 3 * MB // 4, 2)), jnp.arange(MB), side="right"))(jax.random.split(own_keys[4], MICRO * GROUPS)).reshape((MICRO, GROUPS, MB)).astype(jnp.int32)
    out_proj = scatter_about(streams_of[5], (HEADS * HD, D), (HEADS * HD) ** -0.5, 0.09375, ((0, 4), (1, 4)))
    norm_gain = jnp.clip(1.0 + 0.18 * jax.random.normal(streams_of[6], (D,), jnp.float32), 0.1, 1.9)
    router = scatter_about(streams_of[7], (D, EXPERTS), D ** -0.5, 0.09375)
    routes_keys = jax.random.split(jax.random.fold_in(own_keys[8], 1), MICRO * GROUPS * MB // MB_TOK)
    routes_turns = jax.random.permutation(jax.random.fold_in(own_keys[8], 3), MICRO * GROUPS * MB // MB_TOK)
    routes = jax.vmap(lambda own, number: assign_block(jax.random.fold_in(own_keys[8], 2), own, number, MB_TOK, EXPERTS, TOPK, CAP, 2))(routes_keys, routes_turns).reshape((MICRO, GROUPS, MB, TOPK))
    gate_proj = scatter_about(streams_of[9], (2 * EXPERTS, D, HALF), D ** -0.5, 0.09375, ((0, 16),))
    up_proj = scatter_about(streams_of[10], (2 * EXPERTS, D, HALF), D ** -0.5, 0.09375, ((0, 16),))
    down_proj = scatter_about(streams_of[11], (2 * EXPERTS, HALF, D), FF ** -0.5, 0.21875, ((0, 16),))
    return {"stream": stream, "queries": queries, "key_rows": key_rows, "value_rows": value_rows, "segments": segments, "out_proj": out_proj, "norm_gain": norm_gain, "router": router, "routes": routes, "gate_proj": gate_proj, "up_proj": up_proj, "down_proj": down_proj}


epsilon = 1e-06

def attend_block(operands, out_proj):
    query_block, key_block, value_block, segment_ids = operands
    head_map = np.arange(HEADS) // (HEADS // KV)
    query_heads = query_block.reshape(MB, HEADS, HD).astype(jnp.float32)
    key_heads = key_block.reshape(MB, KV, HD).astype(jnp.float32)[:, head_map]
    value_heads = value_block.reshape(MB, KV, HD).astype(jnp.float32)[:, head_map]
    scores = jnp.einsum('qhd,khd->hqk', query_heads, key_heads, precision=lax.Precision.HIGHEST) * (1.0 / math.sqrt(HD))
    positions = jnp.arange(MB)
    allowed = (segment_ids[:, None] == segment_ids[None, :]) & (positions[None, :] <= positions[:, None])
    masked = jnp.where(allowed[None], scores, -1e+30)
    largest = lax.optimization_barrier(jnp.max(masked, axis=-1, keepdims=True))
    powered = jnp.where(allowed[None], jnp.exp(masked - largest), 0.0)
    probs = (powered / lax.optimization_barrier(jnp.sum(powered, axis=-1, keepdims=True))).astype(jnp.bfloat16)
    attended = jnp.einsum('hqk,khd->qhd', probs.astype(jnp.float32), value_heads, precision=lax.Precision.HIGHEST).astype(jnp.bfloat16)
    width = HEADS * HD // N_TENSOR
    pieces = attended.reshape(MB, N_TENSOR, width).astype(jnp.float32)
    proj_groups = out_proj.reshape(N_TENSOR, width, D).astype(jnp.float32)
    head_sums = jnp.einsum('qgw,gwd->gqd', pieces, proj_groups, precision=lax.Precision.HIGHEST).astype(jnp.bfloat16)
    head_sums = lax.optimization_barrier(head_sums)
    return lax.optimization_barrier(jnp.sum(head_sums.astype(jnp.float32), axis=0))

def reference(stream, queries, key_rows, value_rows, segments, out_proj, norm_gain, router, routes, gate_proj, up_proj, down_proj):
    blocks = MICRO * GROUPS
    total = blocks * MB
    attn_out = lax.map(partial(attend_block, out_proj=out_proj), (queries.reshape(blocks, MB, HEADS * HD), key_rows.reshape(blocks, MB, KV * HD), value_rows.reshape(blocks, MB, KV * HD), segments.reshape(blocks, MB)))
    residual = stream.reshape(total, D).astype(jnp.float32) + attn_out.reshape(total, D)
    scale = lax.rsqrt(lax.optimization_barrier(jnp.mean(residual * residual, axis=-1, keepdims=True)) + epsilon)
    normed = (residual * scale * norm_gain).astype(jnp.bfloat16)
    logits = jnp.dot(normed, router, preferred_element_type=jnp.float32)
    chosen = routes.reshape(total, TOPK).astype(jnp.int32)
    picked = jnp.take_along_axis(logits, chosen, axis=1)
    mixing = 1.0 / lax.optimization_barrier(jnp.sum(jnp.exp(picked[:, None, :] - picked[:, :, None]), axis=-1))
    copy_ids = chosen.reshape(-1)
    limit = CAP * MICRO * GROUPS * N_TENSOR
    padded = jnp.concatenate([normed, jnp.zeros((1, D), jnp.bfloat16)], axis=0)

    def serve(expert, table):
        found = jnp.nonzero(copy_ids == expert, size=limit, fill_value=total * TOPK)[0].astype(jnp.int32)
        rows_in = padded[found // TOPK]
        halves = []
        for half in range(2):
            index = 2 * expert + half
            gate_val = jnp.dot(rows_in, gate_proj[index], preferred_element_type=jnp.float32)
            up_val = jnp.dot(rows_in, up_proj[index], preferred_element_type=jnp.float32)
            hidden = (jax.nn.silu(gate_val) * up_val).astype(jnp.bfloat16)
            halves.append(jnp.dot(hidden, down_proj[index], preferred_element_type=jnp.float32).astype(jnp.bfloat16))
        paired = lax.optimization_barrier(tuple(halves))
        summed = (paired[0].astype(jnp.float32) + paired[1].astype(jnp.float32)).astype(jnp.bfloat16)
        return table.at[found].set(summed)
    table = lax.fori_loop(0, EXPERTS, serve, jnp.zeros((total * TOPK + 1, D), jnp.bfloat16))
    expert_out = table[:total * TOPK].reshape(total, TOPK, D).astype(jnp.float32)
    mixed = residual + lax.optimization_barrier(jnp.sum(mixing[:, :, None] * expert_out, axis=1))
    return mixed.astype(jnp.bfloat16).reshape(MICRO, GROUPS, MB, D)
```

```python
import math

import jax
import jax.numpy as jnp
from jax import lax
from jax.sharding import Mesh, PartitionSpec as P

HEADS = 32
KV = 2
HD = 128
TOPK = 2
SWAP = ((0, 1), (1, 0))
CHIPS = ("expert", "x")
TENSOR = ("x", "core")


epsilon = 1e-06


def attend_rows(query_block, key_all, value_all, segment_ids, kv_head):
    seq_rows = key_all.shape[0]
    heads_here = query_block.shape[-1] // HD
    key_head = lax.dynamic_slice_in_dim(key_all, kv_head * HD, HD, 1)
    value_head = lax.dynamic_slice_in_dim(value_all, kv_head * HD, HD, 1)
    query_heads = query_block.reshape(seq_rows, heads_here, HD)
    scores = jnp.einsum(
        "qhd,kd->hqk", query_heads, key_head, preferred_element_type=jnp.float32
    ) * (1.0 / math.sqrt(HD))
    positions = lax.broadcasted_iota(jnp.int32, (seq_rows, seq_rows), 0)
    columns = lax.broadcasted_iota(jnp.int32, (seq_rows, seq_rows), 1)
    allowed = (segment_ids[:, None] == segment_ids[None, :]) & (columns <= positions)
    masked = jnp.where(allowed[None], scores, -1e30)
    largest = jnp.max(masked, axis=-1, keepdims=True)
    powered = jnp.where(allowed[None], jnp.exp(masked - largest), 0.0)
    probs = (powered / jnp.sum(powered, axis=-1, keepdims=True)).astype(jnp.bfloat16)
    attended = jnp.einsum("hqk,kd->qhd", probs, value_head, preferred_element_type=jnp.float32)
    return attended.astype(jnp.bfloat16).reshape(seq_rows, heads_here * HD)


def expert_rows(rows_in, gate_w, up_w, down_w):
    flat_rows = rows_in.reshape(-1, rows_in.shape[-1])
    gate_val = jnp.dot(flat_rows, gate_w, preferred_element_type=jnp.float32)
    up_val = jnp.dot(flat_rows, up_w, preferred_element_type=jnp.float32)
    hidden = (jax.nn.silu(gate_val) * up_val).astype(jnp.bfloat16)
    result = jnp.dot(hidden, down_w, preferred_element_type=jnp.float32).astype(jnp.bfloat16)
    return result.reshape(rows_in.shape)


def local(
    stream,
    queries,
    key_rows,
    value_rows,
    segments,
    out_proj,
    norm_gain,
    router,
    routes,
    gate_proj,
    up_proj,
    down_proj,
):
    f32 = jnp.float32
    bf16 = jnp.bfloat16
    tensor_index = lax.axis_index(TENSOR)
    group_index = lax.axis_index("group")
    core_index = lax.axis_index("core")
    x_index = lax.axis_index("x")
    n_groups = lax.axis_size("group")
    n_x = lax.axis_size("x")
    micros = stream.shape[0]
    heads_here = queries.shape[-1] // HD
    kv_head = tensor_index * heads_here // (HEADS // KV)
    tok_rows = stream.shape[2]
    model_width = stream.shape[3]
    n_experts = router.shape[1]
    capacity = max(2, 3 * tok_rows * TOPK // (2 * n_experts))
    gate_w = gate_proj[0]
    up_w = up_proj[0]
    down_w = down_proj[0]
    proj_rows, proj_cols = out_proj.shape
    piece_rows = proj_rows // n_groups
    piece = lax.dynamic_slice_in_dim(out_proj, group_index * piece_rows, piece_rows, 0)
    pieces = lax.all_gather(piece, ("group", "expert"), axis=0, tiled=False)
    pieces = pieces.reshape(n_groups, -1, piece_rows, proj_cols)
    kv_width = key_rows.shape[-1]
    kv_all = lax.all_gather(
        jnp.concatenate([key_rows[:, 0], value_rows[:, 0]], axis=-1), TENSOR, axis=1, tiled=True
    )

    def project(rows):
        split_rows = rows.reshape(rows.shape[0], n_groups, piece_rows)
        return jnp.einsum(
            "tgk,gekn->ten", split_rows, pieces, preferred_element_type=f32
        ).reshape(rows.shape[0], model_width).astype(bf16)

    results = []
    for micro in range(micros):
        attended = attend_rows(
            queries[micro, 0],
            kv_all[micro, :, :kv_width],
            kv_all[micro, :, kv_width:],
            segments[micro, 0],
            kv_head,
        )
        by_core = attended.reshape(n_x, 2, tok_rows, attended.shape[-1])
        theirs = lax.dynamic_index_in_dim(by_core, 1 - core_index, 1, keepdims=False)
        mine = lax.dynamic_index_in_dim(by_core, core_index, 1, keepdims=False)
        theirs = project(theirs.reshape(n_x * tok_rows, -1))
        arrived = lax.ppermute(theirs, "core", SWAP)
        mine = project(mine.reshape(n_x * tok_rows, -1))
        on_chip = (mine.astype(f32) + arrived.astype(f32)).astype(bf16)
        if n_x == 2:
            by_x = on_chip.reshape(n_x, tok_rows, model_width)
            away = lax.dynamic_index_in_dim(by_x, 1 - x_index, 0, keepdims=False)
            here = lax.dynamic_index_in_dim(by_x, x_index, 0, keepdims=False)
            attn_out = here.astype(f32) + lax.ppermute(away, "x", SWAP).astype(f32)
        else:
            attn_out = lax.psum_scatter(
                on_chip, "x", scatter_dimension=0, tiled=True
            ).astype(f32)
        residual = stream[micro, 0].astype(f32) + attn_out
        scale = lax.rsqrt(jnp.mean(residual * residual, axis=-1, keepdims=True) + epsilon)
        normed = (residual * scale * norm_gain).astype(bf16)
        logits = jnp.dot(normed, router, preferred_element_type=f32)
        chosen = routes[micro, 0]
        expert_iota = lax.broadcasted_iota(jnp.int32, (1, 1, n_experts), 2)
        picks = chosen[:, :, None] == expert_iota
        picked = jnp.sum(jnp.where(picks, logits[:, None, :], 0.0), axis=-1)
        mixing = 1.0 / jnp.sum(jnp.exp(picked[:, None, :] - picked[:, :, None]), axis=-1)
        named = jnp.sum(picks.astype(bf16), axis=1)
        before = (
            lax.broadcasted_iota(jnp.int32, (tok_rows, tok_rows), 1)
            < lax.broadcasted_iota(jnp.int32, (tok_rows, tok_rows), 0)
        ).astype(bf16)
        slots = jnp.dot(before, named, preferred_element_type=f32).astype(jnp.int32)
        slot_hot = (
            slots[:, :, None] == lax.broadcasted_iota(jnp.int32, (1, 1, capacity), 2)
        ) & (named[:, :, None] > 0)
        placing = slot_hot.astype(bf16)
        expert_mix = jnp.sum(jnp.where(picks, mixing[:, :, None], 0.0), axis=1)
        mix_hot = jnp.where(slot_hot, expert_mix[:, :, None], 0.0)
        mix_high = mix_hot.astype(bf16)
        mix_low = (mix_hot - mix_high.astype(f32)).astype(bf16)
        packed = jnp.einsum("tec,td->ecd", placing, normed, preferred_element_type=f32).astype(bf16)
        own_rows = lax.all_to_all(packed, CHIPS, split_axis=0, concat_axis=0, tiled=True)
        sibling_rows = lax.ppermute(own_rows, "core", SWAP)
        sibling_out = expert_rows(sibling_rows, gate_w, up_w, down_w)
        sibling_half = lax.ppermute(sibling_out, "core", SWAP)
        own_out = expert_rows(own_rows, gate_w, up_w, down_w)
        summed = (own_out.astype(f32) + sibling_half.astype(f32)).astype(bf16)
        returned = lax.all_to_all(summed, CHIPS, split_axis=0, concat_axis=0, tiled=True)
        mixed = (
            residual
            + jnp.einsum("tec,ecd->td", mix_high, returned, preferred_element_type=f32)
            + jnp.einsum("tec,ecd->td", mix_low, returned, preferred_element_type=f32)
        )
        results.append(mixed.astype(bf16))
    return jnp.stack(results)[:, None]


def solution(mesh):
    n_group, n_expert, n_tensor = (mesh.shape[axis] for axis in ("group", "expert", "tensor"))
    fine = Mesh(
        mesh.devices.reshape(n_group, n_expert, n_tensor // 2, 2), ("group", "expert", "x", "core")
    )
    requests = ("group", "expert")
    rows = P(None, requests, TENSOR, None)
    halves = P(("expert", "x", "core"), None, None)
    return jax.shard_map(
        local,
        mesh=fine,
        in_specs=(
            rows,
            P(None, requests, None, TENSOR),
            rows,
            rows,
            P(None, requests, None),
            P(TENSOR, "expert"),
            P(),
            P(),
            rows,
            halves,
            halves,
            halves,
        ),
        out_specs=rows,
        check_vma=False,
    )
```

```python
import functools
import math

import jax
import jax.numpy as jnp
from jax import lax
from jax.experimental import pallas as pl
from jax.experimental.pallas import tpu as pltpu
from jax.sharding import Mesh, PartitionSpec as P

HEADS = 32
KV = 2
HD = 128
TOPK = 2
SWAP = ((0, 1), (1, 0))
CHIPS = ("expert", "x")
TENSOR = ("x", "core")


epsilon = 1e-06


def attend_rows(query_block, key_all, value_all, segment_ids, kv_head):
    seq_rows = key_all.shape[0]
    heads_here = query_block.shape[-1] // HD
    key_head = lax.dynamic_slice_in_dim(key_all, kv_head * HD, HD, 1)
    value_head = lax.dynamic_slice_in_dim(value_all, kv_head * HD, HD, 1)
    query_heads = query_block.reshape(seq_rows, heads_here, HD)
    scores = jnp.einsum(
        "qhd,kd->hqk", query_heads, key_head, preferred_element_type=jnp.float32
    ) * (1.0 / math.sqrt(HD))
    positions = lax.broadcasted_iota(jnp.int32, (seq_rows, seq_rows), 0)
    columns = lax.broadcasted_iota(jnp.int32, (seq_rows, seq_rows), 1)
    allowed = (segment_ids[:, None] == segment_ids[None, :]) & (columns <= positions)
    masked = jnp.where(allowed[None], scores, -1e30)
    largest = jnp.max(masked, axis=-1, keepdims=True)
    powered = jnp.where(allowed[None], jnp.exp(masked - largest), 0.0)
    probs = (powered / jnp.sum(powered, axis=-1, keepdims=True)).astype(jnp.bfloat16)
    attended = jnp.einsum("hqk,kd->qhd", probs, value_head, preferred_element_type=jnp.float32)
    return attended.astype(jnp.bfloat16).reshape(seq_rows, heads_here * HD)


def experts_kernel(
    n_chunks,
    rows_ref,
    gate_ref,
    up_ref,
    down_ref,
    out_ref,
    mine,
    theirs,
    part_out,
    part_in,
    row_send,
    row_recv,
    part_send,
    part_recv,
):
    sibling = {"core": 1 - lax.axis_index("core")}
    n_blocks, block_rows, width = rows_ref.shape
    stride = mine.shape[0] // n_blocks
    chunk_blocks = n_blocks // n_chunks
    chunk_rows = chunk_blocks * stride
    whole_rows = block_rows // 16 * 16
    barrier = pltpu.get_barrier_semaphore()
    pl.semaphore_signal(barrier, inc=1, device_id=sibling, device_id_type=pl.DeviceIdType.MESH)

    def stage(chunk):
        for block in range(chunk * chunk_blocks, (chunk + 1) * chunk_blocks):
            base = block * stride
            if whole_rows:
                mine[base : base + whole_rows] = rows_ref[block, :whole_rows]
            if whole_rows < block_rows:
                rest = rows_ref[block, whole_rows:].astype(jnp.float32)
                filler = jnp.zeros((16 - block_rows + whole_rows, width), jnp.float32)
                mine[base + whole_rows : base + stride] = jnp.concatenate(
                    [rest, filler], axis=0
                ).astype(jnp.bfloat16)

    def send(source, target, send_sem, recv_sem, chunk):
        part = pl.ds(chunk * chunk_rows, chunk_rows)
        return pltpu.make_async_remote_copy(
            src_ref=source.at[part],
            dst_ref=target.at[part],
            send_sem=send_sem.at[chunk],
            recv_sem=recv_sem.at[chunk],
            device_id=sibling,
            device_id_type=pl.DeviceIdType.MESH,
        )

    def hidden_of(source, chunk):
        rows = source[chunk * chunk_rows : (chunk + 1) * chunk_rows]
        gate_val = jnp.dot(rows, gate_ref[...], preferred_element_type=jnp.float32)
        up_val = jnp.dot(rows, up_ref[...], preferred_element_type=jnp.float32)
        return (gate_val / (1.0 + jnp.exp(-gate_val)) * up_val).astype(jnp.bfloat16)

    tile = min(width, 1024)
    row_copies = [send(mine, theirs, row_send, row_recv, chunk) for chunk in range(n_chunks)]
    part_copies = [send(part_out, part_in, part_send, part_recv, c) for c in range(n_chunks)]
    for chunk in range(n_chunks):
        stage(chunk)
        if chunk == 0:
            pl.semaphore_wait(barrier, 1)
        row_copies[chunk].start()
    for chunk in range(n_chunks):
        row_copies[chunk].wait_recv()
        hidden = hidden_of(theirs, chunk)
        for column in range(0, width, tile):
            part_out[chunk * chunk_rows : (chunk + 1) * chunk_rows, column : column + tile] = (
                jnp.dot(
                    hidden,
                    down_ref[:, column : column + tile],
                    preferred_element_type=jnp.float32,
                ).astype(jnp.bfloat16)
            )
        part_copies[chunk].start()
    for chunk in range(n_chunks):
        hidden = hidden_of(mine, chunk)
        part_copies[chunk].wait_recv()
        for column in range(0, width, tile):
            here = jnp.dot(
                hidden, down_ref[:, column : column + tile], preferred_element_type=jnp.float32
            ).astype(jnp.bfloat16)
            other = part_in[chunk * chunk_rows : (chunk + 1) * chunk_rows, column : column + tile]
            both = (here.astype(jnp.float32) + other.astype(jnp.float32)).astype(jnp.bfloat16)
            for block in range(chunk_blocks):
                out_ref[chunk * chunk_blocks + block, :, column : column + tile] = both[
                    block * stride : block * stride + block_rows
                ]
    for chunk in range(n_chunks):
        row_copies[chunk].wait_send()
        part_copies[chunk].wait_send()


def run_experts(rows_in, gate_w, up_w, down_w):
    given = rows_in.shape
    width = given[-1]
    if given[1] < 16:
        rows_in = rows_in.reshape(-1, given[1] * (16 // given[1]), width)
    n_blocks, block_rows, _ = rows_in.shape
    stride = -(-block_rows // 16) * 16
    n_chunks = 2
    buffer = pltpu.VMEM((n_blocks * stride, width), jnp.bfloat16)
    sems = pltpu.SemaphoreType.DMA((n_chunks,))
    result = pl.pallas_call(
        functools.partial(experts_kernel, n_chunks),
        out_shape=jax.ShapeDtypeStruct(rows_in.shape, jnp.bfloat16),
        in_specs=[pl.BlockSpec(memory_space=pltpu.VMEM)] * 4,
        out_specs=pl.BlockSpec(memory_space=pltpu.VMEM),
        scratch_shapes=[buffer] * 4 + [sems] * 4,
        compiler_params=pltpu.CompilerParams(
            collective_id=0, has_side_effects=True, vmem_limit_bytes=44 * 1024 * 1024
        ),
        cost_estimate=pl.CostEstimate(
            flops=12 * n_blocks * block_rows * width * gate_w.shape[1],
            bytes_accessed=2 * (3 * width * gate_w.shape[1] + 6 * n_blocks * block_rows * width),
            transcendentals=0,
        ),
    )(rows_in, gate_w, up_w, down_w)
    return result.reshape(given)


def local(
    stream,
    queries,
    key_rows,
    value_rows,
    segments,
    out_proj,
    norm_gain,
    router,
    routes,
    gate_proj,
    up_proj,
    down_proj,
):
    f32 = jnp.float32
    bf16 = jnp.bfloat16
    tensor_index = lax.axis_index(TENSOR)
    group_index = lax.axis_index("group")
    core_index = lax.axis_index("core")
    x_index = lax.axis_index("x")
    n_groups = lax.axis_size("group")
    n_x = lax.axis_size("x")
    micros = stream.shape[0]
    heads_here = queries.shape[-1] // HD
    kv_head = tensor_index * heads_here // (HEADS // KV)
    tok_rows = stream.shape[2]
    model_width = stream.shape[3]
    n_experts = router.shape[1]
    capacity = max(2, 3 * tok_rows * TOPK // (2 * n_experts))
    gate_w = gate_proj[0]
    up_w = up_proj[0]
    down_w = down_proj[0]
    proj_rows, proj_cols = out_proj.shape
    piece_rows = proj_rows // n_groups
    piece = lax.dynamic_slice_in_dim(out_proj, group_index * piece_rows, piece_rows, 0)
    pieces = lax.all_gather(piece, ("group", "expert"), axis=0, tiled=False)
    pieces = pieces.reshape(n_groups, -1, piece_rows, proj_cols)
    kv_width = key_rows.shape[-1]
    kv_all = lax.all_gather(
        jnp.concatenate([key_rows[:, 0], value_rows[:, 0]], axis=-1), TENSOR, axis=1, tiled=True
    )

    def project(rows):
        split_rows = rows.reshape(rows.shape[0], n_groups, piece_rows)
        return jnp.einsum(
            "tgk,gekn->ten", split_rows, pieces, preferred_element_type=f32
        ).reshape(rows.shape[0], model_width).astype(bf16)

    results = []
    for micro in range(micros):
        attended = attend_rows(
            queries[micro, 0],
            kv_all[micro, :, :kv_width],
            kv_all[micro, :, kv_width:],
            segments[micro, 0],
            kv_head,
        )
        by_core = attended.reshape(n_x, 2, tok_rows, attended.shape[-1])
        theirs = lax.dynamic_index_in_dim(by_core, 1 - core_index, 1, keepdims=False)
        mine = lax.dynamic_index_in_dim(by_core, core_index, 1, keepdims=False)
        theirs = project(theirs.reshape(n_x * tok_rows, -1))
        arrived = lax.ppermute(theirs, "core", SWAP)
        mine = project(mine.reshape(n_x * tok_rows, -1))
        on_chip = (mine.astype(f32) + arrived.astype(f32)).astype(bf16)
        if n_x == 2:
            by_x = on_chip.reshape(n_x, tok_rows, model_width)
            away = lax.dynamic_index_in_dim(by_x, 1 - x_index, 0, keepdims=False)
            here = lax.dynamic_index_in_dim(by_x, x_index, 0, keepdims=False)
            attn_out = here.astype(f32) + lax.ppermute(away, "x", SWAP).astype(f32)
        else:
            attn_out = lax.psum_scatter(
                on_chip, "x", scatter_dimension=0, tiled=True
            ).astype(f32)
        residual = stream[micro, 0].astype(f32) + attn_out
        scale = lax.rsqrt(jnp.mean(residual * residual, axis=-1, keepdims=True) + epsilon)
        normed = (residual * scale * norm_gain).astype(bf16)
        logits = jnp.dot(normed, router, preferred_element_type=f32)
        chosen = routes[micro, 0]
        expert_iota = lax.broadcasted_iota(jnp.int32, (1, 1, n_experts), 2)
        picks = chosen[:, :, None] == expert_iota
        picked = jnp.sum(jnp.where(picks, logits[:, None, :], 0.0), axis=-1)
        mixing = 1.0 / jnp.sum(jnp.exp(picked[:, None, :] - picked[:, :, None]), axis=-1)
        named = jnp.sum(picks.astype(bf16), axis=1)
        before = (
            lax.broadcasted_iota(jnp.int32, (tok_rows, tok_rows), 1)
            < lax.broadcasted_iota(jnp.int32, (tok_rows, tok_rows), 0)
        ).astype(bf16)
        slots = jnp.dot(before, named, preferred_element_type=f32).astype(jnp.int32)
        slot_hot = (
            slots[:, :, None] == lax.broadcasted_iota(jnp.int32, (1, 1, capacity), 2)
        ) & (named[:, :, None] > 0)
        placing = slot_hot.astype(bf16)
        expert_mix = jnp.sum(jnp.where(picks, mixing[:, :, None], 0.0), axis=1)
        mix_hot = jnp.where(slot_hot, expert_mix[:, :, None], 0.0)
        mix_high = mix_hot.astype(bf16)
        mix_low = (mix_hot - mix_high.astype(f32)).astype(bf16)
        packed = jnp.einsum("tec,td->ecd", placing, normed, preferred_element_type=f32).astype(bf16)
        own_rows = lax.all_to_all(packed, CHIPS, split_axis=0, concat_axis=0, tiled=True)
        summed = run_experts(own_rows, gate_w, up_w, down_w)
        returned = lax.all_to_all(summed, CHIPS, split_axis=0, concat_axis=0, tiled=True)
        mixed = (
            residual
            + jnp.einsum("tec,ecd->td", mix_high, returned, preferred_element_type=f32)
            + jnp.einsum("tec,ecd->td", mix_low, returned, preferred_element_type=f32)
        )
        results.append(mixed.astype(bf16))
    return jnp.stack(results)[:, None]


def solution(mesh):
    n_group, n_expert, n_tensor = (mesh.shape[axis] for axis in ("group", "expert", "tensor"))
    fine = Mesh(
        mesh.devices.reshape(n_group, n_expert, n_tensor // 2, 2), ("group", "expert", "x", "core")
    )
    requests = ("group", "expert")
    rows = P(None, requests, TENSOR, None)
    halves = P(("expert", "x", "core"), None, None)
    return jax.shard_map(
        local,
        mesh=fine,
        in_specs=(
            rows,
            P(None, requests, None, TENSOR),
            rows,
            rows,
            P(None, requests, None),
            P(TENSOR, "expert"),
            P(),
            P(),
            rows,
            halves,
            halves,
            halves,
        ),
        out_specs=rows,
        check_vma=False,
    )
```

```python
import functools
import math

import jax
import jax.numpy as jnp
from jax import lax
from jax.experimental import pallas as pl
from jax.experimental.pallas import tpu as pltpu
from jax.sharding import Mesh, PartitionSpec as P

HEADS = 32
KV = 2
HD = 128
TOPK = 2
SWAP = ((0, 1), (1, 0))
CHIPS = ("expert", "x")
TENSOR = ("x", "core")


epsilon = 1e-06


def attend_rows(query_block, key_all, value_all, segment_ids, kv_head):
    seq_rows = key_all.shape[0]
    heads_here = query_block.shape[-1] // HD
    key_head = lax.dynamic_slice_in_dim(key_all, kv_head * HD, HD, 1)
    value_head = lax.dynamic_slice_in_dim(value_all, kv_head * HD, HD, 1)
    query_heads = query_block.reshape(seq_rows, heads_here, HD)
    scores = jnp.einsum(
        "qhd,kd->hqk", query_heads, key_head, preferred_element_type=jnp.float32
    ) * (1.0 / math.sqrt(HD))
    positions = lax.broadcasted_iota(jnp.int32, (seq_rows, seq_rows), 0)
    columns = lax.broadcasted_iota(jnp.int32, (seq_rows, seq_rows), 1)
    allowed = (segment_ids[:, None] == segment_ids[None, :]) & (columns <= positions)
    masked = jnp.where(allowed[None], scores, -1e30)
    largest = jnp.max(masked, axis=-1, keepdims=True)
    powered = jnp.where(allowed[None], jnp.exp(masked - largest), 0.0)
    probs = (powered / jnp.sum(powered, axis=-1, keepdims=True)).astype(jnp.bfloat16)
    attended = jnp.einsum("hqk,kd->qhd", probs, value_head, preferred_element_type=jnp.float32)
    return attended.astype(jnp.bfloat16).reshape(seq_rows, heads_here * HD)


def experts_kernel(
    n_chunks,
    rows_ref,
    gate_ref,
    up_ref,
    down_ref,
    out_ref,
    mine,
    theirs,
    part_out,
    part_in,
    row_send,
    row_recv,
    part_send,
    part_recv,
):
    sibling = {"core": 1 - lax.axis_index("core")}
    n_blocks, block_rows, width = rows_ref.shape
    stride = mine.shape[0] // n_blocks
    chunk_blocks = n_blocks // n_chunks
    chunk_rows = chunk_blocks * stride
    whole_rows = block_rows // 16 * 16
    barrier = pltpu.get_barrier_semaphore()
    pl.semaphore_signal(barrier, inc=1, device_id=sibling, device_id_type=pl.DeviceIdType.MESH)

    def stage(chunk):
        for block in range(chunk * chunk_blocks, (chunk + 1) * chunk_blocks):
            base = block * stride
            if whole_rows:
                mine[base : base + whole_rows] = rows_ref[block, :whole_rows]
            if whole_rows < block_rows:
                rest = rows_ref[block, whole_rows:].astype(jnp.float32)
                filler = jnp.zeros((16 - block_rows + whole_rows, width), jnp.float32)
                mine[base + whole_rows : base + stride] = jnp.concatenate(
                    [rest, filler], axis=0
                ).astype(jnp.bfloat16)

    def send(source, target, send_sem, recv_sem, chunk):
        part = pl.ds(chunk * chunk_rows, chunk_rows)
        return pltpu.make_async_remote_copy(
            src_ref=source.at[part],
            dst_ref=target.at[part],
            send_sem=send_sem.at[chunk],
            recv_sem=recv_sem.at[chunk],
            device_id=sibling,
            device_id_type=pl.DeviceIdType.MESH,
        )

    def hidden_of(source, chunk):
        rows = source[chunk * chunk_rows : (chunk + 1) * chunk_rows]
        gate_val = jnp.dot(rows, gate_ref[...], preferred_element_type=jnp.float32)
        up_val = jnp.dot(rows, up_ref[...], preferred_element_type=jnp.float32)
        return (gate_val / (1.0 + jnp.exp(-gate_val)) * up_val).astype(jnp.bfloat16)

    tile = min(width, 1024)
    row_copies = [send(mine, theirs, row_send, row_recv, chunk) for chunk in range(n_chunks)]
    part_copies = [send(part_out, part_in, part_send, part_recv, c) for c in range(n_chunks)]
    for chunk in range(n_chunks):
        stage(chunk)
        if chunk == 0:
            pl.semaphore_wait(barrier, 1)
        row_copies[chunk].start()
    for chunk in range(n_chunks):
        row_copies[chunk].wait_recv()
        hidden = hidden_of(theirs, chunk)
        for column in range(0, width, tile):
            part_out[chunk * chunk_rows : (chunk + 1) * chunk_rows, column : column + tile] = (
                jnp.dot(
                    hidden,
                    down_ref[:, column : column + tile],
                    preferred_element_type=jnp.float32,
                ).astype(jnp.bfloat16)
            )
        part_copies[chunk].start()
    for chunk in range(n_chunks):
        hidden = hidden_of(mine, chunk)
        part_copies[chunk].wait_recv()
        for column in range(0, width, tile):
            here = jnp.dot(
                hidden, down_ref[:, column : column + tile], preferred_element_type=jnp.float32
            ).astype(jnp.bfloat16)
            other = part_in[chunk * chunk_rows : (chunk + 1) * chunk_rows, column : column + tile]
            both = (here.astype(jnp.float32) + other.astype(jnp.float32)).astype(jnp.bfloat16)
            for block in range(chunk_blocks):
                out_ref[chunk * chunk_blocks + block, :, column : column + tile] = both[
                    block * stride : block * stride + block_rows
                ]
    for chunk in range(n_chunks):
        row_copies[chunk].wait_send()
        part_copies[chunk].wait_send()


def run_experts(rows_in, gate_w, up_w, down_w):
    given = rows_in.shape
    width = given[-1]
    if given[1] < 16:
        rows_in = rows_in.reshape(-1, given[1] * (16 // given[1]), width)
    n_blocks, block_rows, _ = rows_in.shape
    stride = -(-block_rows // 16) * 16
    n_chunks = 2
    buffer = pltpu.VMEM((n_blocks * stride, width), jnp.bfloat16)
    sems = pltpu.SemaphoreType.DMA((n_chunks,))
    result = pl.pallas_call(
        functools.partial(experts_kernel, n_chunks),
        out_shape=jax.ShapeDtypeStruct(rows_in.shape, jnp.bfloat16),
        in_specs=[pl.BlockSpec(memory_space=pltpu.VMEM)] * 4,
        out_specs=pl.BlockSpec(memory_space=pltpu.VMEM),
        scratch_shapes=[buffer] * 4 + [sems] * 4,
        compiler_params=pltpu.CompilerParams(
            collective_id=0, has_side_effects=True, vmem_limit_bytes=44 * 1024 * 1024
        ),
        cost_estimate=pl.CostEstimate(
            flops=12 * n_blocks * block_rows * width * gate_w.shape[1],
            bytes_accessed=2 * (3 * width * gate_w.shape[1] + 6 * n_blocks * block_rows * width),
            transcendentals=0,
        ),
    )(rows_in, gate_w, up_w, down_w)
    return result.reshape(given)


def gather_kernel(n_line, n_subs, own_ref, out_ref, local_sem, right_send, left_send, line_recv, y_send, y_recv):
    place = lax.axis_index("expert")
    group = lax.axis_index("group")
    rows, columns = own_ref.shape
    half = rows // 2
    sub_rows = half // n_subs
    mesh_ids = pl.DeviceIdType.MESH
    right, left = {"expert": place + 1}, {"expert": place - 1}
    other = {"group": 1 - group}
    has_right, has_left = place < n_line - 1, place > 0
    barrier = pltpu.get_barrier_semaphore()
    pl.semaphore_signal(barrier, inc=1, device_id=other, device_id_type=mesh_ids)

    @pl.when(has_right)
    def _():
        pl.semaphore_signal(barrier, inc=1, device_id=right, device_id_type=mesh_ids)

    @pl.when(has_left)
    def _():
        pl.semaphore_signal(barrier, inc=1, device_id=left, device_id_type=mesh_ids)

    peers = 1 + jnp.where(has_right, 1, 0) + jnp.where(has_left, 1, 0)
    pl.semaphore_wait(barrier, peers)

    def spot(side, origin, sub):
        start = pl.multiple_of(side * half + sub * sub_rows, sub_rows)
        return out_ref.at[
            pl.ds(start, sub_rows), pl.ds(pl.multiple_of(origin * columns, columns), columns)
        ]

    def along(origin, sub, target, send_sem, from_own):
        source = spot(group, origin, sub)
        if from_own:
            start = pl.multiple_of(group * half + sub * sub_rows, sub_rows)
            source = own_ref.at[pl.ds(start, sub_rows)]
        return pltpu.make_async_remote_copy(
            src_ref=source,
            dst_ref=spot(group, origin, sub),
            send_sem=send_sem.at[origin, sub],
            recv_sem=line_recv.at[origin, sub],
            device_id=target,
            device_id_type=mesh_ids,
        )

    def across(side, origin, sub):
        return pltpu.make_async_remote_copy(
            src_ref=spot(side, origin, sub),
            dst_ref=spot(side, origin, sub),
            send_sem=y_send.at[origin, sub],
            recv_sem=y_recv.at[origin, sub],
            device_id=other,
            device_id_type=mesh_ids,
        )

    for sub in range(n_subs):
        pl.when(has_right)(lambda sub=sub: along(place, sub, right, right_send, True).start())
        pl.when(has_left)(lambda sub=sub: along(place, sub, left, left_send, True).start())
    own_place = out_ref.at[:, pl.ds(pl.multiple_of(place * columns, columns), columns)]
    keep = pltpu.make_async_copy(own_ref, own_place, local_sem)
    keep.start()

    def pass_on(origin, sub, onward, target, send_sem):
        along(origin, sub, target, send_sem, False).wait_recv()
        pl.when(onward)(lambda: along(origin, sub, target, send_sem, False).start())
        across(group, origin, sub).start()

    def finish(origin, sub, onward, target, send_sem):
        pl.when(onward)(lambda: along(origin, sub, target, send_sem, False).wait_send())
        across(group, origin, sub).wait_send()
        across(1 - group, origin, sub).wait_recv()

    for act in (pass_on, finish):
        for distance in range(1, n_line):
            for sub in range(n_subs):
                pl.when(place >= distance)(
                    lambda: act(place - distance, sub, has_right, right, right_send)
                )
                pl.when(place + distance < n_line)(
                    lambda: act(place + distance, sub, has_left, left, left_send)
                )
    for sub in range(n_subs):
        pl.when(has_right)(lambda sub=sub: along(place, sub, right, right_send, True).wait_send())
        pl.when(has_left)(lambda sub=sub: along(place, sub, left, left_send, True).wait_send())
    keep.wait()


def gather_projection(out_proj):
    n_line = lax.axis_size("expert")
    rows, columns = out_proj.shape
    n_subs = 2
    sems = pltpu.SemaphoreType.DMA((n_line, n_subs))
    return pl.pallas_call(
        functools.partial(gather_kernel, n_line, n_subs),
        out_shape=jax.ShapeDtypeStruct((rows, columns * n_line), jnp.bfloat16),
        in_specs=[pl.BlockSpec(memory_space=pl.ANY)],
        out_specs=pl.BlockSpec(memory_space=pl.ANY),
        scratch_shapes=[pltpu.SemaphoreType.DMA] + [sems] * 5,
        compiler_params=pltpu.CompilerParams(collective_id=1, has_side_effects=True),
        cost_estimate=pl.CostEstimate(
            flops=0, bytes_accessed=4 * rows * columns * n_line, transcendentals=0
        ),
    )(out_proj)


def local(
    stream,
    queries,
    key_rows,
    value_rows,
    segments,
    out_proj,
    norm_gain,
    router,
    routes,
    gate_proj,
    up_proj,
    down_proj,
):
    f32 = jnp.float32
    bf16 = jnp.bfloat16
    tensor_index = lax.axis_index(TENSOR)
    core_index = lax.axis_index("core")
    x_index = lax.axis_index("x")
    n_x = lax.axis_size("x")
    micros = stream.shape[0]
    heads_here = queries.shape[-1] // HD
    kv_head = tensor_index * heads_here // (HEADS // KV)
    tok_rows = stream.shape[2]
    model_width = stream.shape[3]
    n_experts = router.shape[1]
    capacity = max(2, 3 * tok_rows * TOPK // (2 * n_experts))
    gate_w = gate_proj[0]
    up_w = up_proj[0]
    down_w = down_proj[0]
    proj_full = gather_projection(out_proj)
    kv_width = key_rows.shape[-1]
    kv_all = lax.all_gather(
        jnp.concatenate([key_rows[:, 0], value_rows[:, 0]], axis=-1), TENSOR, axis=1, tiled=True
    )

    def project(rows):
        return jnp.dot(rows, proj_full, preferred_element_type=f32).astype(bf16)

    results = []
    for micro in range(micros):
        attended = attend_rows(
            queries[micro, 0],
            kv_all[micro, :, :kv_width],
            kv_all[micro, :, kv_width:],
            segments[micro, 0],
            kv_head,
        )
        by_core = attended.reshape(n_x, 2, tok_rows, attended.shape[-1])
        theirs = lax.dynamic_index_in_dim(by_core, 1 - core_index, 1, keepdims=False)
        mine = lax.dynamic_index_in_dim(by_core, core_index, 1, keepdims=False)
        theirs = project(theirs.reshape(n_x * tok_rows, -1))
        arrived = lax.ppermute(theirs, "core", SWAP)
        mine = project(mine.reshape(n_x * tok_rows, -1))
        on_chip = (mine.astype(f32) + arrived.astype(f32)).astype(bf16)
        if n_x == 2:
            by_x = on_chip.reshape(n_x, tok_rows, model_width)
            away = lax.dynamic_index_in_dim(by_x, 1 - x_index, 0, keepdims=False)
            here = lax.dynamic_index_in_dim(by_x, x_index, 0, keepdims=False)
            attn_out = here.astype(f32) + lax.ppermute(away, "x", SWAP).astype(f32)
        else:
            attn_out = lax.psum_scatter(
                on_chip, "x", scatter_dimension=0, tiled=True
            ).astype(f32)
        residual = stream[micro, 0].astype(f32) + attn_out
        scale = lax.rsqrt(jnp.mean(residual * residual, axis=-1, keepdims=True) + epsilon)
        normed = (residual * scale * norm_gain).astype(bf16)
        logits = jnp.dot(normed, router, preferred_element_type=f32)
        chosen = routes[micro, 0]
        expert_iota = lax.broadcasted_iota(jnp.int32, (1, 1, n_experts), 2)
        picks = chosen[:, :, None] == expert_iota
        picked = jnp.sum(jnp.where(picks, logits[:, None, :], 0.0), axis=-1)
        mixing = 1.0 / jnp.sum(jnp.exp(picked[:, None, :] - picked[:, :, None]), axis=-1)
        named = jnp.sum(picks.astype(bf16), axis=1)
        before = (
            lax.broadcasted_iota(jnp.int32, (tok_rows, tok_rows), 1)
            < lax.broadcasted_iota(jnp.int32, (tok_rows, tok_rows), 0)
        ).astype(bf16)
        slots = jnp.dot(before, named, preferred_element_type=f32).astype(jnp.int32)
        slot_hot = (
            slots[:, :, None] == lax.broadcasted_iota(jnp.int32, (1, 1, capacity), 2)
        ) & (named[:, :, None] > 0)
        placing = slot_hot.astype(bf16)
        expert_mix = jnp.sum(jnp.where(picks, mixing[:, :, None], 0.0), axis=1)
        mix_hot = jnp.where(slot_hot, expert_mix[:, :, None], 0.0)
        mix_high = mix_hot.astype(bf16)
        mix_low = (mix_hot - mix_high.astype(f32)).astype(bf16)
        packed = jnp.einsum("tec,td->ecd", placing, normed, preferred_element_type=f32).astype(bf16)
        own_rows = lax.all_to_all(packed, CHIPS, split_axis=0, concat_axis=0, tiled=True)
        summed = run_experts(own_rows, gate_w, up_w, down_w)
        returned = lax.all_to_all(summed, CHIPS, split_axis=0, concat_axis=0, tiled=True)
        mixed = (
            residual
            + jnp.einsum("tec,ecd->td", mix_high, returned, preferred_element_type=f32)
            + jnp.einsum("tec,ecd->td", mix_low, returned, preferred_element_type=f32)
        )
        results.append(mixed.astype(bf16))
    return jnp.stack(results)[:, None]


def solution(mesh):
    n_group, n_expert, n_tensor = (mesh.shape[axis] for axis in ("group", "expert", "tensor"))
    fine = Mesh(
        mesh.devices.reshape(n_group, n_expert, n_tensor // 2, 2), ("group", "expert", "x", "core")
    )
    requests = ("group", "expert")
    rows = P(None, requests, TENSOR, None)
    halves = P(("expert", "x", "core"), None, None)
    return jax.shard_map(
        local,
        mesh=fine,
        in_specs=(
            rows,
            P(None, requests, None, TENSOR),
            rows,
            rows,
            P(None, requests, None),
            P(TENSOR, "expert"),
            P(),
            P(),
            rows,
            halves,
            halves,
            halves,
        ),
        out_specs=rows,
        check_vma=False,
    )
```
